512 devices in a mesh: cfg: 2 (over z_lo), section: 8 (over z_hi, core), patch: 32 (over x, y).
Axes of the slice: x: 4, y: 8, z: 8 (z_hi: 4, z_lo: 2; z = z_hi * 2 + z_lo), core: 2. Of those that a mesh axis runs over, the one named last changes fastest.
Arguments:
- inputs: bfloat16 [2, 1024, 1536], P('cfg', 'patch'), may hold values from -6 to 6
- stale_kv: bfloat16 [2, 8, 2, 1024, 1536], P('cfg', 'section', None, 'patch'), may hold values from -6 to 6
- q_gain: float32 [8, 1536], P('section'), may hold values from 0.3 to 1.2
- k_gain: float32 [8, 1536], P('section'), may hold values from 0.3 to 1.2
- v_gain: float32 [8, 1536], P('section'), may hold values from 0.5 to 2
- o_gain: float32 [8, 1536], P('section'), may hold values from 2 to 8
Outputs:
- guided: bfloat16 [1024, 1536], P('patch', ('cfg', 'section'))
- fresh_kv: bfloat16 [2, 8, 2, 1024, 1536], P('cfg', 'section', None, 'patch')
The draws below stay inside these ranges and needn't reach their ends.
All inputs are finite; a program needn't handle non-finite values.
Results may differ from the reference program's by a relative error of at most 0.017.
Values may be sent and summed in bfloat16 or wider, within the bound.
A program may use at most 64 MiB of HBM per device.

```python
import math
import jax
import jax.numpy as jnp
from jax import lax

HEADS = 12
HD = 128
TOK_DEV = 32
MB = 8
HW = 1536
SECTIONS = 8
TOKENS = 1024
N_SECTION = 8
N_PATCH = 32


def steps_of(key, dims, cuts, low, high):
    factor_of = 1.0
    for axis_at, blocks in cuts:
        heights = jax.random.uniform(jax.random.fold_in(jax.random.fold_in(key, 6), axis_at), (blocks,), jnp.float32, low / len(cuts), high / len(cuts))
        factor_of = factor_of * jnp.repeat(jnp.exp(heights), dims[axis_at] // blocks).reshape((-1,) + (1,) * (len(dims) - 1 - axis_at))
    return factor_of


def noise(own_key, dims, deviation, most, shards=(), kind=jnp.bfloat16):
    array = jax.random.normal(own_key, dims, jnp.float32) * deviation
    if len(shards) > 0:
        array = steps_of(own_key, dims, shards, -0.22, 0.18) * array
    return jnp.clip(array, min=-most, max=most).astype(kind)


def setup_inputs(seed: int = 0) -> dict:
    streams_of = jax.random.split(jax.random.key(seed), 7)
    inputs = noise(streams_of[0], (2, TOKENS, HW), 1.0, 6.0, ((0, 2), (1, 32)))
    stale_kv = noise(streams_of[1], (2, SECTIONS, 2, TOKENS, HW), 1.0, 6.0, ((0, 2), (1, 8), (3, 32)))
    q_gain = jnp.clip(jnp.exp(math.log(1.2) - 1.3862944 * jax.random.uniform(streams_of[2], (SECTIONS, HW), jnp.float32) ** steps_of(streams_of[2], (SECTIONS, HW), ((0, 8),), -0.2, 0.2)), 0.3, 1.2)
    k_gain = jnp.clip(jnp.exp(math.log(1.2) - 1.3862944 * jax.random.uniform(streams_of[3], (SECTIONS, HW), jnp.float32) ** steps_of(streams_of[3], (SECTIONS, HW), ((0, 8),), -0.2, 0.2)), 0.3, 1.2)
    v_gain = jnp.clip(jnp.exp(math.log(2.0) - 1.3862944 * jax.random.uniform(streams_of[4], (SECTIONS, HW), jnp.float32) ** steps_of(streams_of[4], (SECTIONS, HW), ((0, 8),), -0.2, 0.2)), 0.5, 2.0)
    o_gain = jnp.clip(jnp.exp(math.log(8.0) - 1.3862944 * jax.random.uniform(streams_of[5], (SECTIONS, HW), jnp.float32) ** steps_of(streams_of[5], (SECTIONS, HW), ((0, 8),), -0.2, 0.2)), 2.0, 8.0)
    return {"inputs": inputs, "stale_kv": stale_kv, "q_gain": q_gain, "k_gain": k_gain, "v_gain": v_gain, "o_gain": o_gain}


guide_scale = 6.0

def prepare(block, q_row, k_row, v_row):
    rows = block.shape[0]
    wide = block.astype(jnp.float32)
    split = wide.reshape(rows, HEADS, HD)
    normed = split * lax.rsqrt(lax.optimization_barrier(jnp.mean(split * split, axis=2, keepdims=True)) + 1e-06)
    normed = normed.reshape(rows, HEADS * HD)
    query = (normed * q_row).astype(jnp.bfloat16)
    key = (normed * k_row).astype(jnp.bfloat16)
    value = (wide * v_row).astype(jnp.bfloat16)
    return (query, key, value)

def attend_full(query, keys, values):
    rows = query.shape[0]
    count = keys.shape[0]
    q_heads = query.astype(jnp.float32).reshape(rows, HEADS, HD)
    k_heads = keys.astype(jnp.float32).reshape(count, HEADS, HD)
    v_heads = values.astype(jnp.float32).reshape(count, HEADS, HD)
    scores = jnp.einsum('rhd,nhd->hrn', q_heads, k_heads) * HD ** (-0.5)
    top = lax.optimization_barrier(jnp.max(scores, axis=2, keepdims=True))
    expo = jnp.exp(scores - top)
    total = lax.optimization_barrier(jnp.sum(expo, axis=2, keepdims=True))
    weights = (expo / total).astype(jnp.bfloat16).astype(jnp.float32)
    mixed = jnp.einsum('hrn,nhd->rhd', weights, v_heads)
    return mixed.reshape(rows, HEADS * HD)

def reference(inputs, stale_kv, q_gain, k_gain, v_gain, o_gain):
    width = HEADS * HD
    blk = TOK_DEV // MB
    streams = []
    freshes = []
    for branch in range(2):
        stream = inputs[branch].reshape(N_PATCH, TOK_DEV, width)
        section_fresh = []
        for level in range(N_SECTION):
            stale_keys = stale_kv[branch, level, 0]
            stale_vals = stale_kv[branch, level, 1]
            buf_keys = stale_keys.reshape(N_PATCH, TOK_DEV, width)
            buf_vals = stale_vals.reshape(N_PATCH, TOK_DEV, width)
            for micro in range(MB):
                lower = micro * blk
                block = stream[:, lower:lower + blk]
                query, key, value = prepare(block.reshape(N_PATCH * blk, width), q_gain[level], k_gain[level], v_gain[level])
                query = query.reshape(N_PATCH, blk, width)
                buf_keys = buf_keys.at[:, lower:lower + blk].set(key.reshape(N_PATCH, blk, width))
                buf_vals = buf_vals.at[:, lower:lower + blk].set(value.reshape(N_PATCH, blk, width))

                def one_patch(items):
                    q_part, k_part, v_part, owner = items
                    anchor = (owner * TOK_DEV).astype(jnp.int32)
                    zero_index = jnp.zeros((), jnp.int32)
                    keys = lax.dynamic_update_slice(stale_keys, k_part, (anchor, zero_index))
                    values = lax.dynamic_update_slice(stale_vals, v_part, (anchor, zero_index))
                    return attend_full(q_part, keys, values)
                mixed = lax.map(one_patch, (query, buf_keys, buf_vals, jnp.arange(N_PATCH, dtype=jnp.int32)))
                result = (block.astype(jnp.float32) + o_gain[level] * mixed).astype(jnp.bfloat16)
                stream = stream.at[:, lower:lower + blk].set(result)
            section_fresh.append(jnp.stack([buf_keys.reshape(TOK_DEV * N_PATCH, width), buf_vals.reshape(TOK_DEV * N_PATCH, width)]))
        streams.append(stream.reshape(TOK_DEV * N_PATCH, width))
        freshes.append(jnp.stack(section_fresh))
    uncond = streams[0].astype(jnp.float32)
    cond = streams[1].astype(jnp.float32)
    guided = (uncond + guide_scale * (cond - uncond)).astype(jnp.bfloat16)
    return (guided, jnp.stack(freshes))
```

```python
import functools
import math

import jax
import jax.numpy as jnp
from jax import lax
from jax.experimental import pallas as pl
from jax.experimental.pallas import tpu as pltpu
from jax.sharding import PartitionSpec as P

MESH = pl.DeviceIdType.MESH
HD = 128
MB = 8
PARTS = 2
CHUNKS = 2
SHIFT = 24.0
EPS = 1e-6
guide_scale = 6.0


def dot_nt(a, b):
    return lax.dot_general(a, b, (((1,), (1,)), ((), ())), preferred_element_type=jnp.float32)


def dot_nn(a, b):
    return lax.dot_general(a, b, (((1,), (0,)), ((), ())), preferred_element_type=jnp.float32)


def tiles(start, size):
    return pl.ds(pl.multiple_of(start, size), size)


def flow(
    dims, x_ref, kv_ref, qg, kg, vg, og, fs_ref, fin_ref,
    kvb, xin, xmid, xout, gb, mask,
    kv_send, x_send, g_send, nxt_send, ret_send, fin_send,
    kv_sem, xin_sem, g_sem, fs_sem, fin_sem,
):
    heads, n_sec, n_patch, tok, width, nd, slots = dims
    half = n_patch // PARTS
    rows = xin.shape[1]
    per_chunk = rows // tok
    n_tok = n_patch * tok
    blocks = n_tok // rows
    last = n_sec // 2 - 1
    out_w = width // (2 * n_sec)
    c, s, p = lax.axis_index("cfg"), lax.axis_index("section"), lax.axis_index("patch")
    zh = s // 2
    core = lax.rem(s, 2)
    s0 = zh * 2
    part = p // half
    local = lax.rem(p, half)
    head = local - local // 4
    has_unit = (lax.rem(local, 4) != 3) & (head < heads)
    is_unit = has_unit & (core == 0)
    unit_part = PARTS - 1 - part
    col = c * n_sec + s
    h_first = (out_w * col) // HD
    h_last = (out_w * col + out_w - 1) // HD
    as_int = lambda flag: flag.astype(jnp.int32)

    def owner(h, r):
        return (PARTS - 1 - r) * half + h + h // 3

    gains = (qg, kg, vg, og)

    bar = pltpu.get_barrier_semaphore()

    def hello(dev):
        pl.semaphore_signal(bar, inc=1, device_id=dev, device_id_type=MESH)

    @pl.when(is_unit)
    def _():
        for i, g in enumerate(gains):
            pltpu.make_async_copy(g.at[:, tiles(head * HD, HD)], gb.at[0, i], g_sem.at[0]).start()

        def greet(i, _):
            q = lax.rem(p + i, n_patch)

            @pl.when(i > 0)
            def _():
                hello((c, s0, q))

            hello((c, s0 + 1, q))
            return 0

        lax.fori_loop(0, n_patch, greet, 0)

        @pl.when(zh > 0)
        def _():
            hello((c, s0 - 2, p))

    def greet_units(h, _):
        hello((c, s0, owner(h, part)))
        return 0

    lax.fori_loop(0, heads, greet_units, 0)
    for branch in range(2):
        hello((branch, n_sec - 2, owner(h_first, part)))

        @pl.when(h_last > h_first)
        def _():
            hello((branch, n_sec - 2, owner(h_last, part)))

    inner = 2 * half + as_int(zh < last) + as_int(zh == last) * (half * nd)
    pl.semaphore_wait(bar, PARTS * heads + as_int(is_unit) * (inner - 1))

    def g_copy(i):
        return pltpu.make_async_remote_copy(
            src_ref=gains[i].at[:, tiles(head * HD, HD)],
            dst_ref=gb.at[1, i],
            send_sem=g_send.at[i],
            recv_sem=g_sem.at[1],
            device_id=(c, s0, p),
            device_id_type=MESH,
        )

    def x_copy(i):
        h = lax.rem(p + i, heads)
        at = lax.rem(p, half)
        return pltpu.make_async_remote_copy(
            src_ref=x_ref.at[:, tiles(h * HD, HD)],
            dst_ref=xin.at[at // per_chunk, tiles(lax.rem(at, per_chunk) * tok, tok)],
            send_sem=x_send.at[i],
            recv_sem=xin_sem.at[at // per_chunk],
            device_id=(c, 0, owner(h, part)),
            device_id_type=MESH,
        )

    def kv_copy(i):
        k = lax.rem(p + i, PARTS * heads)
        h = lax.rem(k, heads)
        to = owner(h, k // heads)
        src = kv_ref.at[:, :, tiles(h * HD, HD)]
        dst = kvb.at[core, :, tiles(p * tok, tok)]
        mine = (to == p) & (core == 0)
        far = pltpu.make_async_remote_copy(
            src_ref=src,
            dst_ref=dst,
            send_sem=kv_send.at[i],
            recv_sem=kv_sem.at[core],
            device_id=(c, s0, to),
            device_id_type=MESH,
        )
        return mine, src, dst, far

    def x_start(i, _):
        x_copy(i).start()
        return 0

    def kv_start(i, _):
        mine, src, dst, far = kv_copy(i)

        @pl.when(mine)
        def _():
            pltpu.make_async_copy(src, dst, kv_sem.at[0]).start()

        @pl.when(jnp.logical_not(mine))
        def _():
            far.start()

        return 0

    @pl.when(has_unit & (core == 1))
    def _():
        for i in range(4):
            g_copy(i).start()

    @pl.when(s == 0)
    def _():
        lax.fori_loop(0, heads, x_start, 0)

    lax.fori_loop(0, PARTS * heads, kv_start, 0)

    def next_copy(ch):
        return pltpu.make_async_remote_copy(
            src_ref=xout.at[ch],
            dst_ref=xin.at[ch],
            send_sem=nxt_send.at[ch],
            recv_sem=xin_sem.at[ch],
            device_id=(c, s0 + 2, p),
            device_id_type=MESH,
        )

    def ret_copy(ch, sec, i):
        src = (xin, xmid)[sec]
        return pltpu.make_async_remote_copy(
            src_ref=src.at[ch, tiles(i * tok, tok)],
            dst_ref=fs_ref.at[:, tiles(head * HD, HD)],
            send_sem=ret_send.at[ch, sec, i],
            recv_sem=fs_sem,
            device_id=(c, s0 + sec, unit_part * half + ch * per_chunk + i),
            device_id_type=MESH,
        )

    def fin_copy(ch, i, n):
        j = (HD * head) // out_w + n
        slot = head - (out_w * j) // HD
        return pltpu.make_async_remote_copy(
            src_ref=xout.at[ch, tiles(i * tok, tok)],
            dst_ref=fin_ref.at[slot, c],
            send_sem=fin_send.at[ch, i, n],
            recv_sem=fin_sem.at[slot],
            device_id=(j // n_sec, lax.rem(j, n_sec), unit_part * half + ch * per_chunk + i),
            device_id_type=MESH,
        )

    def attend(ch, sec, x):
        row = lambda i: gb[sec, i]
        wide = x.astype(jnp.float32)
        normed = wide * lax.rsqrt(jnp.mean(wide * wide, axis=1, keepdims=True) + EPS)
        query = (normed * row(0)).astype(jnp.bfloat16)
        key = (normed * row(1)).astype(jnp.bfloat16)
        value = (wide * row(2)).astype(jnp.bfloat16)
        near = mask[...] != 0.0
        fresh = dot_nt(query, key)
        diag = unit_part * CHUNKS + ch
        expo = []
        for j in range(blocks):
            at = tiles(lax.rem(diag + j, blocks) * rows, rows)
            score = dot_nt(query, kvb[sec, 0, at])
            if j == 0:
                score = jnp.where(near, fresh, score)
            expo.append(jnp.exp2(score * (HD**-0.5 * math.log2(math.e)) - SHIFT))
        inverse = 1.0 / jnp.sum(sum(expo), axis=1, keepdims=True)
        mixed = None
        for j in range(blocks):
            at = tiles(lax.rem(diag + j, blocks) * rows, rows)
            weight = expo[j] * inverse
            if j == 0:
                mixed = dot_nn(jnp.where(near, weight, 0.0).astype(jnp.bfloat16), value)
                weight = jnp.where(near, 0.0, weight)
            mixed = mixed + dot_nn(weight.astype(jnp.bfloat16), kvb[sec, 1, at])
        return (wide + row(3) * mixed).astype(jnp.bfloat16)

    @pl.when(is_unit)
    def _():
        r = lax.broadcasted_iota(jnp.int32, (rows, rows), 0)
        t = lax.broadcasted_iota(jnp.int32, (rows, rows), 1)
        blk = tok // MB
        seen = (r // tok == t // tok) & (t // blk <= r // blk)
        mask[...] = jnp.where(seen, 1.0, 0.0)

        for ch in range(CHUNKS):
            pltpu.make_async_copy(xin.at[ch], xin.at[ch], xin_sem.at[ch]).wait()
            if ch == 0:
                pltpu.make_async_copy(gb.at[0], gb.at[0], g_sem.at[0]).wait()
                pltpu.make_async_copy(kvb.at[0], kvb.at[0], kv_sem.at[0]).wait()
            xmid[ch] = attend(ch, 0, xin[ch])
            if ch == 0:
                pltpu.make_async_copy(gb.at[1], gb.at[1], g_sem.at[1]).wait()
                pltpu.make_async_copy(kvb.at[1], kvb.at[1], kv_sem.at[1]).wait()
            xout[ch] = attend(ch, 1, xmid[ch])

            @pl.when(zh < last)
            def _():
                next_copy(ch).start()

            @pl.when(zh == last)
            def _():
                def fin_start(i, _):
                    for n in range(nd):
                        fin_copy(ch, i, n).start()
                    return 0

                lax.fori_loop(0, per_chunk, fin_start, 0)

            def ret_start(i, _):
                for sec in range(2):
                    ret_copy(ch, sec, i).start()
                return 0

            lax.fori_loop(0, per_chunk, ret_start, 0)

        for ch in range(CHUNKS):

            @pl.when(zh < last)
            def _():
                next_copy(ch).wait_send()

            @pl.when(zh == last)
            def _():
                def fin_wait(i, _):
                    for n in range(nd):
                        fin_copy(ch, i, n).wait_send()
                    return 0

                lax.fori_loop(0, per_chunk, fin_wait, 0)

            def ret_wait(i, _):
                for sec in range(2):
                    ret_copy(ch, sec, i).wait_send()
                return 0

            lax.fori_loop(0, per_chunk, ret_wait, 0)

    @pl.when(has_unit & (core == 1))
    def _():
        for i in range(4):
            g_copy(i).wait_send()

    def x_wait(i, _):
        x_copy(i).wait_send()
        return 0

    def kv_wait(i, _):
        mine, _, _, far = kv_copy(i)

        @pl.when(jnp.logical_not(mine))
        def _():
            far.wait_send()

        return 0

    @pl.when(s == 0)
    def _():
        lax.fori_loop(0, heads, x_wait, 0)

    lax.fori_loop(0, PARTS * heads, kv_wait, 0)
    pltpu.make_async_copy(fs_ref, fs_ref, fs_sem).wait()
    pltpu.make_async_copy(fin_ref.at[0], fin_ref.at[0], fin_sem.at[0]).wait()
    if slots == 2:

        @pl.when(h_last > h_first)
        def _():
            pltpu.make_async_copy(fin_ref.at[1], fin_ref.at[1], fin_sem.at[1]).wait()

        @pl.when(h_last == h_first)
        def _():
            fin_ref[1] = jnp.zeros(fin_ref.shape[1:], fin_ref.dtype)


def finish(dims, fs_ref, fin_ref, kg, vg, guided_ref, fresh_ref):
    heads, n_sec, n_patch, tok, width, nd, slots = dims
    out_w = width // (2 * n_sec)
    for h in range(heads):
        at = slice(h * HD, (h + 1) * HD)
        wide = fs_ref[:, at].astype(jnp.float32)
        normed = wide * lax.rsqrt(jnp.mean(wide * wide, axis=1, keepdims=True) + EPS)
        fresh_ref[0, :, at] = (normed * kg[:, at]).astype(jnp.bfloat16)
        fresh_ref[1, :, at] = (wide * vg[:, at]).astype(jnp.bfloat16)
    parts = []
    for slot in range(slots):
        uncond = fin_ref[slot, 0].astype(jnp.float32)
        cond = fin_ref[slot, 1].astype(jnp.float32)
        parts.append(uncond + guide_scale * (cond - uncond))
    both = jnp.concatenate(parts, axis=1) if slots == 2 else parts[0]
    col = lax.axis_index("cfg") * n_sec + lax.axis_index("section")
    off = lax.rem(out_w * col, HD)
    for start in sorted({(out_w * j) % HD for j in range(2 * n_sec)}):

        @pl.when(off == start)
        def _():
            guided_ref[...] = both[:, start : start + out_w].astype(jnp.bfloat16)


def local(dims, inputs, stale_kv, q_gain, k_gain, v_gain, o_gain):
    heads, n_sec, n_patch, tok, width, nd, slots = dims
    rows = n_patch * tok // (PARTS * CHUNKS)
    per_chunk = rows // tok
    dma = pltpu.SemaphoreType.DMA
    bf16 = jnp.bfloat16
    vmem = pl.BlockSpec(memory_space=pltpu.VMEM)
    far = pl.BlockSpec(memory_space=pl.ANY)
    fs, fin = pl.pallas_call(
        functools.partial(flow, dims),
        out_shape=(
            jax.ShapeDtypeStruct((tok, width), bf16),
            jax.ShapeDtypeStruct((slots, 2, tok, HD), bf16),
        ),
        in_specs=[far] * 6,
        out_specs=(vmem, vmem),
        scratch_shapes=[
            pltpu.VMEM((2, 2, n_patch * tok, HD), bf16),
            pltpu.VMEM((CHUNKS, rows, HD), bf16),
            pltpu.VMEM((CHUNKS, rows, HD), bf16),
            pltpu.VMEM((CHUNKS, rows, HD), bf16),
            pltpu.VMEM((2, 4, 1, HD), jnp.float32),
            pltpu.VMEM((rows, rows), jnp.float32),
            dma((PARTS * heads,)),
            dma((heads,)),
            dma((4,)),
            dma((CHUNKS,)),
            dma((CHUNKS, 2, per_chunk)),
            dma((CHUNKS, per_chunk, nd)),
            dma((2,)),
            dma((CHUNKS,)),
            dma((2,)),
            dma(()),
            dma((slots,)),
        ],
        compiler_params=pltpu.CompilerParams(collective_id=1, has_side_effects=True),
        name="flow",
    )(inputs[0], stale_kv[0, 0], q_gain, k_gain, v_gain, o_gain)
    guided, fresh = pl.pallas_call(
        functools.partial(finish, dims),
        out_shape=(
            jax.ShapeDtypeStruct((tok, width // (2 * n_sec)), bf16),
            jax.ShapeDtypeStruct((2, tok, width), bf16),
        ),
        in_specs=[vmem] * 4,
        out_specs=(vmem, vmem),
        name="finish",
    )(fs, fin, k_gain, v_gain)
    return guided, fresh[None, None]


def solution(mesh):
    n_cfg, n_sec, n_patch = mesh.shape["cfg"], mesh.shape["section"], mesh.shape["patch"]
    placed = (
        P("cfg", "patch", None),
        P("cfg", "section", None, "patch", None),
        P("section", None),
        P("section", None),
        P("section", None),
        P("section", None),
    )

    def whole(inputs, stale_kv, q_gain, k_gain, v_gain, o_gain):
        tok, width = inputs.shape[1] // n_patch, inputs.shape[2]
        heads = width // HD
        out_w = width // (n_cfg * n_sec)
        takers = {(HD * h + HD - 1) // out_w - (HD * h) // out_w + 1 for h in range(heads)}
        assert len(takers) == 1 and n_cfg == 2
        spans = [(out_w * j + out_w - 1) // HD - (out_w * j) // HD for j in range(n_cfg * n_sec)]
        dims = (heads, n_sec, n_patch, tok, width, takers.pop(), 1 + max(spans))
        return jax.shard_map(
            functools.partial(local, dims),
            mesh=mesh,
            in_specs=placed,
            out_specs=(P("patch", ("cfg", "section")), P("cfg", "section", None, "patch", None)),
            check_vma=False,
        )(inputs, stale_kv, q_gain, k_gain, v_gain, o_gain)

    return whole
```

```python
import functools
import math

import jax
import jax.numpy as jnp
from jax import lax
from jax.experimental import pallas as pl
from jax.experimental.pallas import tpu as pltpu
from jax.sharding import PartitionSpec as P

MESH = pl.DeviceIdType.MESH
HD = 128
MB = 8
PARTS = 4
CHUNKS = 2
SHIFT = 24.0
EPS = 1e-6
guide_scale = 6.0


def dot_nt(a, b):
    return lax.dot_general(a, b, (((1,), (1,)), ((), ())), preferred_element_type=jnp.float32)


def dot_nn(a, b):
    return lax.dot_general(a, b, (((1,), (0,)), ((), ())), preferred_element_type=jnp.float32)


def tiles(start, size):
    return pl.ds(pl.multiple_of(start, size), size)


def flow(
    dims, x_ref, kv_ref, qg, kg, vg, og, fs_ref, fin_ref,
    kvb, xin, xmid, xout, gb, mask,
    kv_send, x_send, g_send, nxt_send, ret_send, fin_send,
    kv_sem, xin_sem, g_sem, fs_sem, fin_sem, rel_send, rel_sem, ret_ok, nxt_ok,
):
    heads, n_sec, n_patch, tok, width, nd, slots = dims
    quarter = n_patch // PARTS
    rows = xin.shape[1]
    per_chunk = rows // tok
    wide_keys = mask.shape[2]
    copies = wide_keys // rows
    blocks = n_patch * tok // wide_keys
    last = n_sec // 2 - 1
    out_w = width // (2 * n_sec)
    ny = 8 if n_patch == 32 else 2
    nx = n_patch // ny
    hy = ny // 2
    c, s, p = lax.axis_index("cfg"), lax.axis_index("section"), lax.axis_index("patch")
    zh = s // 2
    core = lax.rem(s, 2)
    s0 = zh * 2
    as_int = lambda flag: flag.astype(jnp.int32)

    def patch_at(pos):
        at = lax.rem(pos, 2 * quarter)
        return (at // hy) * ny + (pos // (2 * quarter)) * hy + lax.rem(at, hy)

    def owner(h, side, branch):
        at = lax.rem(h, hy)
        return lax.rem(at + branch + 1 + h // hy, nx) * ny + side * hy + at

    x, y = p // ny, lax.rem(p, ny)
    side, at_y = y // hy, lax.rem(y, hy)
    place = x * hy + at_y
    on_core = place // quarter
    place = lax.rem(place, quarter)
    nth = lax.rem(x - at_y - c - 1 + 2 * nx + hy * nx, nx)
    is_unit = nth < heads // hy
    head = lax.rem(nth * hy + at_y, heads)
    block_at = side * 2 + core
    col = c * n_sec + s
    h_first = (out_w * col) // HD
    h_last = (out_w * col + out_w - 1) // HD
    is_final = is_unit & (zh == last)
    gains = (qg, kg, vg, og)

    bar = pltpu.get_barrier_semaphore()
    other = s0 + 1 - core

    def hello(dev):
        pl.semaphore_signal(bar, inc=1, device_id=dev, device_id_type=MESH)

    def loop(n, body, first=0):
        def step(i, _):
            body(i)
            return 0

        lax.fori_loop(first, n, step, 0)

    @pl.when(is_unit)
    def _():
        def greet(i):
            q = lax.rem(p + i, n_patch)
            hello((c, s, q))

            @pl.when((lax.rem(q, ny) // hy == side) & (q // ny // (nx // 2) == core))
            def _():
                hello((c, other, q))

        hello((c, other, p))
        loop(n_patch, greet, 1)

        @pl.when(zh < last)
        def _():
            hello((c, s + 2, p))

        for i, g in enumerate(gains):
            pltpu.make_async_copy(g.at[:, tiles(head * HD, HD)], gb.at[core, i], g_sem.at[0]).start()

    for branch in range(2):
        for n in range(slots):
            h = (h_first, h_last)[n]
            wanted = jnp.logical_not(is_final & (on_core == core) & (c == branch) & (head == h))
            if n == 1:
                wanted = wanted & (h_last > h_first)

            @pl.when(wanted)
            def _():
                hello((branch, n_sec - 2 + on_core, owner(h, side, branch)))

    unit = as_int(is_unit)
    mine_too = is_final & (on_core == core) & (head >= h_first) & (head <= h_last)
    greeted = 2 * heads + as_int(on_core != core) * (heads - unit) + as_int(is_unit & (zh > 0))
    pl.semaphore_wait(bar, greeted + as_int(is_final) * (quarter * nd) - as_int(mine_too))

    def g_copy(i):
        return pltpu.make_async_remote_copy(
            src_ref=gains[i].at[:, tiles(head * HD, HD)],
            dst_ref=gb.at[core, i],
            send_sem=g_send.at[i],
            recv_sem=g_sem.at[1],
            device_id=(c, other, p),
            device_id_type=MESH,
        )

    def x_copy(i):
        h = lax.rem(p + i, heads)
        to = owner(h, side, c)
        src = x_ref.at[:, tiles(h * HD, HD)]
        dst = xin.at[place // per_chunk, tiles(lax.rem(place, per_chunk) * tok, tok)]
        far = pltpu.make_async_remote_copy(
            src_ref=src,
            dst_ref=dst,
            send_sem=x_send.at[i],
            recv_sem=xin_sem.at[place // per_chunk],
            device_id=(c, on_core, to),
            device_id_type=MESH,
        )
        return (to == p) & (on_core == 0), src, dst, xin_sem.at[place // per_chunk], far

    def kv_copy(i):
        k = lax.rem(p + i, 2 * heads)
        h = lax.rem(k, heads)
        to = owner(h, k // heads, c)
        at = (side * 2 + on_core) * quarter + place
        src = kv_ref.at[:, :, tiles(h * HD, HD)]
        dst = kvb.at[core, :, tiles(at * tok, tok)]
        sem = kv_sem.at[at * tok // wide_keys]
        far = pltpu.make_async_remote_copy(
            src_ref=src,
            dst_ref=dst,
            send_sem=kv_send.at[i],
            recv_sem=sem,
            device_id=(c, s, to),
            device_id_type=MESH,
        )
        return to == p, src, dst, sem, far

    def relay(i):
        block = kvb.at[core, :, slice(i * wide_keys, (i + 1) * wide_keys)]
        return pltpu.make_async_remote_copy(
            src_ref=block,
            dst_ref=block,
            send_sem=rel_send.at[i],
            recv_sem=rel_sem.at[i],
            device_id=(c, other, p),
            device_id_type=MESH,
        )

    def start(copy):
        mine, src, dst, sem, far = copy

        @pl.when(mine)
        def _():
            pltpu.make_async_copy(src, dst, sem).start()

        @pl.when(jnp.logical_not(mine))
        def _():
            far.start()

    def sent(copy):
        @pl.when(jnp.logical_not(copy[0]))
        def _():
            copy[4].wait_send()

    @pl.when(s == 0)
    def _():
        loop(heads, lambda i: start(x_copy(i)))

    loop(2 * heads, lambda i: start(kv_copy(i)))

    @pl.when(is_unit)
    def _():
        for i in range(4):
            g_copy(i).start()

    def ready(h):
        to = owner(h, side, c)

        @pl.when(jnp.logical_not((to == p) & (on_core == core)))
        def _():
            pl.semaphore_signal(ret_ok, inc=1, device_id=(c, s0 + on_core, to), device_id_type=MESH)

    loop(heads, ready)

    @pl.when(is_unit & (zh > 0))
    def _():
        pl.semaphore_signal(nxt_ok, inc=1, device_id=(c, s - 2, p), device_id_type=MESH)

    def next_copy(ch):
        return pltpu.make_async_remote_copy(
            src_ref=xout.at[ch],
            dst_ref=xin.at[ch],
            send_sem=nxt_send.at[ch],
            recv_sem=xin_sem.at[ch],
            device_id=(c, s + 2, p),
            device_id_type=MESH,
        )

    def ret_copy(ch, sec, i):
        to = patch_at(block_at * quarter + ch * per_chunk + i)
        src = (xin, xmid)[sec].at[ch, tiles(i * tok, tok)]
        dst = fs_ref.at[:, tiles(head * HD, HD)]
        far = pltpu.make_async_remote_copy(
            src_ref=src,
            dst_ref=dst,
            send_sem=ret_send.at[ch, sec, i],
            recv_sem=fs_sem,
            device_id=(c, s0 + sec, to),
            device_id_type=MESH,
        )
        return (to == p) & (core == sec), src, dst, fs_sem, far

    def fin_copy(ch, i, n):
        j = (HD * head) // out_w + n
        slot = head - (out_w * j) // HD
        to = patch_at(block_at * quarter + ch * per_chunk + i)
        src = xout.at[ch, tiles(i * tok, tok)]
        dst = fin_ref.at[slot, c]
        far = pltpu.make_async_remote_copy(
            src_ref=src,
            dst_ref=dst,
            send_sem=fin_send.at[ch, i, n],
            recv_sem=fin_sem.at[slot],
            device_id=(j // n_sec, lax.rem(j, n_sec), to),
            device_id_type=MESH,
        )
        return (to == p) & (j == col), src, dst, fin_sem.at[slot], far

    def attend(ch, sec, x):
        row = lambda i: gb[sec, i]
        wide = x.astype(jnp.float32)
        normed = wide * lax.rsqrt(jnp.mean(wide * wide, axis=1, keepdims=True) + EPS)
        query = (normed * row(0)).astype(jnp.bfloat16)
        key = (normed * row(1)).astype(jnp.bfloat16)
        value = (wide * row(2)).astype(jnp.bfloat16)
        near = mask[ch % copies] != 0.0
        fresh = dot_nt(query, jnp.concatenate([key] * copies, axis=0))
        diag = block_at * (CHUNKS // copies) + ch // copies
        expo = []
        for j in range(blocks):
            at = tiles(lax.rem(diag + j, blocks) * wide_keys, wide_keys)
            score = dot_nt(query, kvb[sec, 0, at])
            if j == 0:
                score = jnp.where(near, fresh, score)
            expo.append(jnp.exp2(score * (HD**-0.5 * math.log2(math.e)) - SHIFT))
        inverse = 1.0 / jnp.sum(sum(expo), axis=1, keepdims=True)
        mixed = None
        for j in range(blocks):
            at = tiles(lax.rem(diag + j, blocks) * wide_keys, wide_keys)
            weight = expo[j] * inverse
            if j == 0:
                mixed = dot_nn(
                    jnp.where(near, weight, 0.0).astype(jnp.bfloat16),
                    jnp.concatenate([value] * copies, axis=0),
                )
                weight = jnp.where(near, 0.0, weight)
            mixed = mixed + dot_nn(weight.astype(jnp.bfloat16), kvb[sec, 1, at])
        return (wide + row(3) * mixed).astype(jnp.bfloat16)

    @pl.when(is_unit)
    def _():
        blk = tok // MB
        for v in range(copies):
            r = lax.broadcasted_iota(jnp.int32, (rows, wide_keys), 0) + v * rows
            t = lax.broadcasted_iota(jnp.int32, (rows, wide_keys), 1)
            seen = (r // tok == t // tok) & (t // blk <= r // blk)
            mask[v] = jnp.where(seen, 1.0, 0.0)

        def relayed():
            for i in range(blocks):
                relay(i).wait_recv()

        for i in range(blocks):
            block = kvb.at[core, :, slice(i * wide_keys, (i + 1) * wide_keys)]
            pltpu.make_async_copy(block, block, kv_sem.at[i]).wait()
            relay(i).start()
        pltpu.make_async_copy(gb.at[0], gb.at[0], g_sem.at[0]).wait()
        pltpu.make_async_copy(gb.at[1], gb.at[1], g_sem.at[1]).wait()

        for ch in range(CHUNKS):
            pltpu.make_async_copy(xin.at[ch], xin.at[ch], xin_sem.at[ch]).wait()
            if ch == 0:
                pl.when(core == 1)(relayed)
            xmid[ch] = attend(ch, 0, xin[ch])
            if ch == 0:
                pl.when(core == 0)(relayed)
            xout[ch] = attend(ch, 1, xmid[ch])

            @pl.when(zh < last)
            def _():
                if ch == 0:
                    pl.semaphore_wait(nxt_ok, 1)
                next_copy(ch).start()

            @pl.when(zh == last)
            def _():
                def go(i):
                    for n in range(nd):
                        start(fin_copy(ch, i, n))

                loop(per_chunk, go)

            if ch == 0:
                pl.semaphore_wait(ret_ok, 2 * quarter - as_int(on_core == core))

            def go(i):
                for sec in range(2):
                    start(ret_copy(ch, sec, i))

            loop(per_chunk, go)

        for ch in range(CHUNKS):

            @pl.when(zh < last)
            def _():
                next_copy(ch).wait_send()

            @pl.when(zh == last)
            def _():
                def go(i):
                    for n in range(nd):
                        sent(fin_copy(ch, i, n))

                loop(per_chunk, go)

            def go(i):
                for sec in range(2):
                    sent(ret_copy(ch, sec, i))

            loop(per_chunk, go)

    @pl.when(is_unit)
    def _():
        for i in range(4):
            g_copy(i).wait_send()
        for i in range(blocks):
            relay(i).wait_send()

    @pl.when(s == 0)
    def _():
        loop(heads, lambda i: sent(x_copy(i)))

    loop(2 * heads, lambda i: sent(kv_copy(i)))
    pltpu.make_async_copy(fs_ref, fs_ref, fs_sem).wait()
    pltpu.make_async_copy(fin_ref.at[0], fin_ref.at[0], fin_sem.at[0]).wait()
    if slots == 2:

        @pl.when(h_last > h_first)
        def _():
            pltpu.make_async_copy(fin_ref.at[1], fin_ref.at[1], fin_sem.at[1]).wait()

        @pl.when(h_last == h_first)
        def _():
            fin_ref[1] = jnp.zeros(fin_ref.shape[1:], fin_ref.dtype)


def finish(dims, fs_ref, fin_ref, kg, vg, guided_ref, fresh_ref):
    heads, n_sec, n_patch, tok, width, nd, slots = dims
    out_w = width // (2 * n_sec)
    for h in range(heads):
        at = slice(h * HD, (h + 1) * HD)
        wide = fs_ref[:, at].astype(jnp.float32)
        normed = wide * lax.rsqrt(jnp.mean(wide * wide, axis=1, keepdims=True) + EPS)
        fresh_ref[0, :, at] = (normed * kg[:, at]).astype(jnp.bfloat16)
        fresh_ref[1, :, at] = (wide * vg[:, at]).astype(jnp.bfloat16)
    parts = []
    for slot in range(slots):
        uncond = fin_ref[slot, 0].astype(jnp.float32)
        cond = fin_ref[slot, 1].astype(jnp.float32)
        parts.append(uncond + guide_scale * (cond - uncond))
    both = jnp.concatenate(parts, axis=1) if slots == 2 else parts[0]
    col = lax.axis_index("cfg") * n_sec + lax.axis_index("section")
    off = lax.rem(out_w * col, HD)
    for start in sorted({(out_w * j) % HD for j in range(2 * n_sec)}):

        @pl.when(off == start)
        def _():
            guided_ref[...] = both[:, start : start + out_w].astype(jnp.bfloat16)


def local(dims, inputs, stale_kv, q_gain, k_gain, v_gain, o_gain):
    heads, n_sec, n_patch, tok, width, nd, slots = dims
    rows = n_patch * tok // (PARTS * CHUNKS)
    per_chunk = rows // tok
    wide_keys = min(256, n_patch * tok // PARTS)
    dma = pltpu.SemaphoreType.DMA
    bf16 = jnp.bfloat16
    vmem = pl.BlockSpec(memory_space=pltpu.VMEM)
    far = pl.BlockSpec(memory_space=pl.ANY)
    fs, fin = pl.pallas_call(
        functools.partial(flow, dims),
        out_shape=(
            jax.ShapeDtypeStruct((tok, width), bf16),
            jax.ShapeDtypeStruct((slots, 2, tok, HD), bf16),
        ),
        in_specs=[far] * 6,
        out_specs=(vmem, vmem),
        scratch_shapes=[
            pltpu.VMEM((2, 2, n_patch * tok, HD), bf16),
            pltpu.VMEM((CHUNKS, rows, HD), bf16),
            pltpu.VMEM((CHUNKS, rows, HD), bf16),
            pltpu.VMEM((CHUNKS, rows, HD), bf16),
            pltpu.VMEM((2, 4, 1, HD), jnp.float32),
            pltpu.VMEM((wide_keys // rows, rows, wide_keys), jnp.float32),
            dma((2 * heads,)),
            dma((heads,)),
            dma((4,)),
            dma((CHUNKS,)),
            dma((CHUNKS, 2, per_chunk)),
            dma((CHUNKS, per_chunk, nd)),
            dma((n_patch * tok // wide_keys,)),
            dma((CHUNKS,)),
            dma((2,)),
            dma(()),
            dma((slots,)),
            dma((n_patch * tok // wide_keys,)),
            dma((n_patch * tok // wide_keys,)),
            pltpu.SemaphoreType.REGULAR,
            pltpu.SemaphoreType.REGULAR,
        ],
        compiler_params=pltpu.CompilerParams(collective_id=1, has_side_effects=True),
        name="flow",
    )(inputs[0], stale_kv[0, 0], q_gain, k_gain, v_gain, o_gain)
    guided, fresh = pl.pallas_call(
        functools.partial(finish, dims),
        out_shape=(
            jax.ShapeDtypeStruct((tok, width // (2 * n_sec)), bf16),
            jax.ShapeDtypeStruct((2, tok, width), bf16),
        ),
        in_specs=[vmem] * 4,
        out_specs=(vmem, vmem),
        name="finish",
    )(fs, fin, k_gain, v_gain)
    return guided, fresh[None, None]


def solution(mesh):
    n_cfg, n_sec, n_patch = mesh.shape["cfg"], mesh.shape["section"], mesh.shape["patch"]
    placed = (
        P("cfg", "patch", None),
        P("cfg", "section", None, "patch", None),
        P("section", None),
        P("section", None),
        P("section", None),
        P("section", None),
    )

    def whole(inputs, stale_kv, q_gain, k_gain, v_gain, o_gain):
        tok, width = inputs.shape[1] // n_patch, inputs.shape[2]
        heads = width // HD
        out_w = width // (n_cfg * n_sec)
        takers = {(HD * h + HD - 1) // out_w - (HD * h) // out_w + 1 for h in range(heads)}
        assert len(takers) == 1 and n_cfg == 2
        spans = [(out_w * j + out_w - 1) // HD - (out_w * j) // HD for j in range(n_cfg * n_sec)]
        dims = (heads, n_sec, n_patch, tok, width, takers.pop(), 1 + max(spans))
        return jax.shard_map(
            functools.partial(local, dims),
            mesh=mesh,
            in_specs=placed,
            out_specs=(P("patch", ("cfg", "section")), P("cfg", "section", None, "patch", None)),
            check_vma=False,
        )(inputs, stale_kv, q_gain, k_gain, v_gain, o_gain)

    return whole
```

```python
import functools
import math

import jax
import jax.numpy as jnp
from jax import lax
from jax.experimental import pallas as pl
from jax.experimental.pallas import tpu as pltpu
from jax.sharding import PartitionSpec as P

MESH = pl.DeviceIdType.MESH
HD = 128
MB = 8
PARTS = 4
CHUNKS = 2
SHIFT = 24.0
EPS = 1e-6
guide_scale = 6.0


def dot_nt(a, b):
    return lax.dot_general(a, b, (((1,), (1,)), ((), ())), preferred_element_type=jnp.float32)


def dot_nn(a, b):
    return lax.dot_general(a, b, (((1,), (0,)), ((), ())), preferred_element_type=jnp.float32)


def tiles(start, size):
    return pl.ds(pl.multiple_of(start, size), size)


def swapped(whole, at, piece):
    parts = [whole[:, : at.start], piece, whole[:, at.stop :]]
    parts = [part for part in parts if part.shape[1]]
    return jnp.concatenate(parts, axis=1) if len(parts) > 1 else piece


def flow(
    dims, x_ref, kv_ref, qg, kg, vg, og, fs_ref, fin_ref,
    kvb, xin, xmid, xout, gb, mask,
    kv_send, x_send, g_send, nxt_send, ret_send, fin_send,
    kv_sem, xin_sem, g_sem, fs_sem, fin_sem, rel_send, rel_sem, ret_ok, nxt_ok,
):
    heads, n_sec, n_patch, tok, width, nd, slots = dims
    quarter = n_patch // PARTS
    rows = xin.shape[1]
    per_chunk = rows // tok
    wide_keys = min(256, n_patch * tok // PARTS)
    copies = wide_keys // rows
    blocks = n_patch * tok // wide_keys
    last = n_sec // 2 - 1
    out_w = width // (2 * n_sec)
    ny = 8 if n_patch == 32 else 2
    nx = n_patch // ny
    hy = ny // 2
    c, s, p = lax.axis_index("cfg"), lax.axis_index("section"), lax.axis_index("patch")
    zh = s // 2
    core = lax.rem(s, 2)
    s0 = zh * 2
    as_int = lambda flag: flag.astype(jnp.int32)

    def patch_at(pos):
        at = lax.rem(pos, 2 * quarter)
        return (at // hy) * ny + (pos // (2 * quarter)) * hy + lax.rem(at, hy)

    def owner(h, side, branch):
        at = lax.rem(h, hy)
        return lax.rem(at + branch + 1 + h // hy, nx) * ny + side * hy + at

    x, y = p // ny, lax.rem(p, ny)
    side, at_y = y // hy, lax.rem(y, hy)
    place = x * hy + at_y
    on_core = place // quarter
    place = lax.rem(place, quarter)
    nth = lax.rem(x - at_y - c - 1 + 2 * nx + hy * nx, nx)
    is_unit = nth < heads // hy
    head = lax.rem(nth * hy + at_y, heads)
    block_at = side * 2 + core
    col = c * n_sec + s
    h_first = (out_w * col) // HD
    h_last = (out_w * col + out_w - 1) // HD
    is_final = is_unit & (zh == last)
    gains = (qg, kg, vg, og)

    bar = pltpu.get_barrier_semaphore()
    other = s0 + 1 - core

    def hello(dev):
        pl.semaphore_signal(bar, inc=1, device_id=dev, device_id_type=MESH)

    def loop(n, body, first=0):
        def step(i, _):
            body(i)
            return 0

        lax.fori_loop(first, n, step, 0)

    @pl.when(is_unit)
    def _():
        def greet(i):
            q = lax.rem(p + i, n_patch)
            hello((c, s, q))

            @pl.when((lax.rem(q, ny) // hy == side) & (q // ny // (nx // 2) == core))
            def _():
                hello((c, other, q))

        hello((c, other, p))
        loop(n_patch, greet, 1)

        @pl.when(zh < last)
        def _():
            hello((c, s + 2, p))

        for i, g in enumerate(gains):
            pltpu.make_async_copy(g.at[:, tiles(head * HD, HD)], gb.at[core, i], g_sem.at[0]).start()

    for branch in range(2):
        for n in range(slots):
            h = (h_first, h_last)[n]
            wanted = jnp.logical_not(is_final & (on_core == core) & (c == branch) & (head == h))
            if n == 1:
                wanted = wanted & (h_last > h_first)

            @pl.when(wanted)
            def _():
                hello((branch, n_sec - 2 + on_core, owner(h, side, branch)))

    unit = as_int(is_unit)
    mine_too = is_final & (on_core == core) & (head >= h_first) & (head <= h_last)
    greeted = 2 * heads + as_int(on_core != core) * (heads - unit) + as_int(is_unit & (zh > 0))
    pl.semaphore_wait(bar, greeted + as_int(is_final) * (quarter * nd) - as_int(mine_too))

    def g_copy(i):
        return pltpu.make_async_remote_copy(
            src_ref=gains[i].at[:, tiles(head * HD, HD)],
            dst_ref=gb.at[core, i],
            send_sem=g_send.at[i],
            recv_sem=g_sem.at[1],
            device_id=(c, other, p),
            device_id_type=MESH,
        )

    def x_copy(i):
        h = lax.rem(p + i, heads)
        to = owner(h, side, c)
        src = x_ref.at[:, tiles(h * HD, HD)]
        dst = xin.at[place // per_chunk, tiles(lax.rem(place, per_chunk) * tok, tok)]
        far = pltpu.make_async_remote_copy(
            src_ref=src,
            dst_ref=dst,
            send_sem=x_send.at[i],
            recv_sem=xin_sem.at[place // per_chunk],
            device_id=(c, on_core, to),
            device_id_type=MESH,
        )
        return (to == p) & (on_core == 0), src, dst, xin_sem.at[place // per_chunk], far

    def kv_copy(i):
        k = lax.rem(p + i, 8)
        h = i // 8 * 2 + lax.rem(k, 2) + lax.rem(k // 2, 2) * (heads // 2)
        to_side = k // 4
        if heads % 6:
            h, to_side = lax.rem(i, heads), i // heads
        to = owner(h, to_side, c)
        at = (side * 2 + on_core) * quarter + place
        src = kv_ref.at[:, :, tiles(h * HD, HD)]
        dst = kvb.at[core, :, tiles(at * tok, tok)]
        sem = kv_sem.at[at * tok // wide_keys]
        far = pltpu.make_async_remote_copy(
            src_ref=src,
            dst_ref=dst,
            send_sem=kv_send.at[i],
            recv_sem=sem,
            device_id=(c, s, to),
            device_id_type=MESH,
        )
        return to == p, src, dst, sem, far

    def relay(i):
        block = kvb.at[core, :, slice(i * wide_keys, (i + 1) * wide_keys)]
        return pltpu.make_async_remote_copy(
            src_ref=block,
            dst_ref=block,
            send_sem=rel_send.at[i],
            recv_sem=rel_sem.at[i],
            device_id=(c, other, p),
            device_id_type=MESH,
        )

    def start(copy):
        mine, src, dst, sem, far = copy

        @pl.when(mine)
        def _():
            pltpu.make_async_copy(src, dst, sem).start()

        @pl.when(jnp.logical_not(mine))
        def _():
            far.start()

    def sent(copy):
        @pl.when(jnp.logical_not(copy[0]))
        def _():
            copy[4].wait_send()

    @pl.when(s == 0)
    def _():
        loop(heads, lambda i: start(x_copy(i)))

    loop(2 * heads, lambda i: start(kv_copy(i)))

    @pl.when(is_unit)
    def _():
        for i in range(4):
            g_copy(i).start()

    def ready(h):
        to = owner(h, side, c)

        @pl.when(jnp.logical_not((to == p) & (on_core == core)))
        def _():
            pl.semaphore_signal(ret_ok, inc=1, device_id=(c, s0 + on_core, to), device_id_type=MESH)

    loop(heads, ready)

    @pl.when(is_unit & (zh > 0))
    def _():
        pl.semaphore_signal(nxt_ok, inc=1, device_id=(c, s - 2, p), device_id_type=MESH)

    def next_copy(ch):
        return pltpu.make_async_remote_copy(
            src_ref=xout.at[ch],
            dst_ref=xin.at[ch],
            send_sem=nxt_send.at[ch],
            recv_sem=xin_sem.at[ch],
            device_id=(c, s + 2, p),
            device_id_type=MESH,
        )

    def ret_copy(ch, sec, i):
        to = patch_at(block_at * quarter + ch * per_chunk + i)
        src = (xin, xmid)[sec].at[ch, tiles(i * tok, tok)]
        dst = fs_ref.at[:, tiles(head * HD, HD)]
        far = pltpu.make_async_remote_copy(
            src_ref=src,
            dst_ref=dst,
            send_sem=ret_send.at[ch, sec, i],
            recv_sem=fs_sem,
            device_id=(c, s0 + sec, to),
            device_id_type=MESH,
        )
        return (to == p) & (core == sec), src, dst, fs_sem, far

    def fin_copy(ch, i, n):
        j = (HD * head) // out_w + n
        slot = head - (out_w * j) // HD
        to = patch_at(block_at * quarter + ch * per_chunk + i)
        src = xout.at[ch, tiles(i * tok, tok)]
        dst = fin_ref.at[slot, c]
        far = pltpu.make_async_remote_copy(
            src_ref=src,
            dst_ref=dst,
            send_sem=fin_send.at[ch, i, n],
            recv_sem=fin_sem.at[slot],
            device_id=(j // n_sec, lax.rem(j, n_sec), to),
            device_id_type=MESH,
        )
        return (to == p) & (j == col), src, dst, fin_sem.at[slot], far

    def attend(ch, sec, x):
        row = lambda i: gb[sec, i]
        wide = x.astype(jnp.float32)
        normed = wide * lax.rsqrt(jnp.mean(wide * wide, axis=1, keepdims=True) + EPS)
        query = (normed * row(0)).astype(jnp.bfloat16)
        key = (normed * row(1)).astype(jnp.bfloat16)
        value = (wide * row(2)).astype(jnp.bfloat16)
        near = mask[...] != 0.0
        fresh = dot_nt(query, key)
        own = slice(ch % copies * rows, (ch % copies + 1) * rows)
        diag = block_at * (CHUNKS // copies) + ch // copies
        expo = []
        for j in range(blocks):
            at = tiles(lax.rem(diag + j, blocks) * wide_keys, wide_keys)
            score = dot_nt(query, kvb[sec, 0, at])
            if j == 0:
                score = swapped(score, own, jnp.where(near, fresh, score[:, own]))
            expo.append(jnp.exp2(score * (HD**-0.5 * math.log2(math.e)) - SHIFT))
        inverse = 1.0 / jnp.sum(sum(expo), axis=1, keepdims=True)
        mixed = None
        for j in range(blocks):
            at = tiles(lax.rem(diag + j, blocks) * wide_keys, wide_keys)
            weight = expo[j] * inverse
            if j == 0:
                mixed = dot_nn(jnp.where(near, weight[:, own], 0.0).astype(jnp.bfloat16), value)
                weight = swapped(weight, own, jnp.where(near, 0.0, weight[:, own]))
            mixed = mixed + dot_nn(weight.astype(jnp.bfloat16), kvb[sec, 1, at])
        return (wide + row(3) * mixed).astype(jnp.bfloat16)

    @pl.when(is_unit)
    def _():
        blk = tok // MB
        r = lax.broadcasted_iota(jnp.int32, (rows, rows), 0)
        t = lax.broadcasted_iota(jnp.int32, (rows, rows), 1)
        seen = (r // tok == t // tok) & (t // blk <= r // blk)
        mask[...] = jnp.where(seen, 1.0, 0.0)

        def relayed():
            for i in range(blocks):
                relay(i).wait_recv()

        for i in range(blocks):
            block = kvb.at[core, :, slice(i * wide_keys, (i + 1) * wide_keys)]
            pltpu.make_async_copy(block, block, kv_sem.at[i]).wait()
            relay(i).start()
        pltpu.make_async_copy(gb.at[0], gb.at[0], g_sem.at[0]).wait()
        pltpu.make_async_copy(gb.at[1], gb.at[1], g_sem.at[1]).wait()

        for ch in range(CHUNKS):
            pltpu.make_async_copy(xin.at[ch], xin.at[ch], xin_sem.at[ch]).wait()
            if ch == 0:
                pl.when(core == 1)(relayed)
            xmid[ch] = attend(ch, 0, xin[ch])
            if ch == 0:
                pl.when(core == 0)(relayed)
            xout[ch] = attend(ch, 1, xmid[ch])

            @pl.when(zh < last)
            def _():
                if ch == 0:
                    pl.semaphore_wait(nxt_ok, 1)
                next_copy(ch).start()

            @pl.when(zh == last)
            def _():
                def go(i):
                    for n in range(nd):
                        start(fin_copy(ch, i, n))

                loop(per_chunk, go)

            if ch == 0:
                pl.semaphore_wait(ret_ok, 2 * quarter - as_int(on_core == core))

            def go(i):
                for sec in range(2):
                    start(ret_copy(ch, sec, i))

            loop(per_chunk, go)

        for ch in range(CHUNKS):

            @pl.when(zh < last)
            def _():
                next_copy(ch).wait_send()

            @pl.when(zh == last)
            def _():
                def go(i):
                    for n in range(nd):
                        sent(fin_copy(ch, i, n))

                loop(per_chunk, go)

            def go(i):
                for sec in range(2):
                    sent(ret_copy(ch, sec, i))

            loop(per_chunk, go)

    @pl.when(is_unit)
    def _():
        for i in range(4):
            g_copy(i).wait_send()
        for i in range(blocks):
            relay(i).wait_send()

    @pl.when(s == 0)
    def _():
        loop(heads, lambda i: sent(x_copy(i)))

    loop(2 * heads, lambda i: sent(kv_copy(i)))
    pltpu.make_async_copy(fs_ref, fs_ref, fs_sem).wait()
    pltpu.make_async_copy(fin_ref.at[0], fin_ref.at[0], fin_sem.at[0]).wait()
    if slots == 2:

        @pl.when(h_last > h_first)
        def _():
            pltpu.make_async_copy(fin_ref.at[1], fin_ref.at[1], fin_sem.at[1]).wait()


def finish(dims, fs_ref, fin_ref, kg, vg, guided_ref, fresh_ref):
    heads, n_sec, n_patch, tok, width, nd, slots = dims
    out_w = width // (2 * n_sec)
    for h in range(heads):
        at = slice(h * HD, (h + 1) * HD)
        wide = fs_ref[:, at].astype(jnp.float32)
        normed = wide * lax.rsqrt(jnp.mean(wide * wide, axis=1, keepdims=True) + EPS)
        fresh_ref[0, :, at] = (normed * kg[:, at]).astype(jnp.bfloat16)
        fresh_ref[1, :, at] = (wide * vg[:, at]).astype(jnp.bfloat16)
    parts = []
    for slot in range(slots):
        uncond = fin_ref[slot, 0].astype(jnp.float32)
        cond = fin_ref[slot, 1].astype(jnp.float32)
        parts.append(uncond + guide_scale * (cond - uncond))
    both = jnp.concatenate(parts, axis=1) if slots == 2 else parts[0]
    col = lax.axis_index("cfg") * n_sec + lax.axis_index("section")
    off = lax.rem(out_w * col, HD)
    for start in sorted({(out_w * j) % HD for j in range(2 * n_sec)}):

        @pl.when(off == start)
        def _():
            guided_ref[...] = both[:, start : start + out_w].astype(jnp.bfloat16)


def local(dims, inputs, stale_kv, q_gain, k_gain, v_gain, o_gain):
    heads, n_sec, n_patch, tok, width, nd, slots = dims
    rows = n_patch * tok // (PARTS * CHUNKS)
    per_chunk = rows // tok
    wide_keys = min(256, n_patch * tok // PARTS)
    dma = pltpu.SemaphoreType.DMA
    bf16 = jnp.bfloat16
    vmem = pl.BlockSpec(memory_space=pltpu.VMEM)
    far = pl.BlockSpec(memory_space=pl.ANY)
    fs, fin = pl.pallas_call(
        functools.partial(flow, dims),
        out_shape=(
            jax.ShapeDtypeStruct((tok, width), bf16),
            jax.ShapeDtypeStruct((slots, 2, tok, HD), bf16),
        ),
        in_specs=[far] * 6,
        out_specs=(far, far),
        scratch_shapes=[
            pltpu.VMEM((2, 2, n_patch * tok, HD), bf16),
            pltpu.VMEM((CHUNKS, rows, HD), bf16),
            pltpu.VMEM((CHUNKS, rows, HD), bf16),
            pltpu.VMEM((CHUNKS, rows, HD), bf16),
            pltpu.VMEM((2, 4, 1, HD), jnp.float32),
            pltpu.VMEM((rows, rows), jnp.float32),
            dma((2 * heads,)),
            dma((heads,)),
            dma((4,)),
            dma((CHUNKS,)),
            dma((CHUNKS, 2, per_chunk)),
            dma((CHUNKS, per_chunk, nd)),
            dma((n_patch * tok // wide_keys,)),
            dma((CHUNKS,)),
            dma((2,)),
            dma(()),
            dma((slots,)),
            dma((n_patch * tok // wide_keys,)),
            dma((n_patch * tok // wide_keys,)),
            pltpu.SemaphoreType.REGULAR,
            pltpu.SemaphoreType.REGULAR,
        ],
        compiler_params=pltpu.CompilerParams(collective_id=1, has_side_effects=True),
        name="flow",
    )(inputs[0], stale_kv[0, 0], q_gain, k_gain, v_gain, o_gain)
    guided, fresh = pl.pallas_call(
        functools.partial(finish, dims),
        out_shape=(
            jax.ShapeDtypeStruct((tok, width // (2 * n_sec)), bf16),
            jax.ShapeDtypeStruct((2, tok, width), bf16),
        ),
        in_specs=[vmem] * 4,
        out_specs=(vmem, vmem),
        name="finish",
    )(fs, fin, k_gain, v_gain)
    return guided, fresh[None, None]


def solution(mesh):
    n_cfg, n_sec, n_patch = mesh.shape["cfg"], mesh.shape["section"], mesh.shape["patch"]
    placed = (
        P("cfg", "patch", None),
        P("cfg", "section", None, "patch", None),
        P("section", None),
        P("section", None),
        P("section", None),
        P("section", None),
    )

    def whole(inputs, stale_kv, q_gain, k_gain, v_gain, o_gain):
        tok, width = inputs.shape[1] // n_patch, inputs.shape[2]
        heads = width // HD
        out_w = width // (n_cfg * n_sec)
        takers = {(HD * h + HD - 1) // out_w - (HD * h) // out_w + 1 for h in range(heads)}
        assert len(takers) == 1 and n_cfg == 2
        spans = [(out_w * j + out_w - 1) // HD - (out_w * j) // HD for j in range(n_cfg * n_sec)]
        dims = (heads, n_sec, n_patch, tok, width, takers.pop(), 1 + max(spans))
        return jax.shard_map(
            functools.partial(local, dims),
            mesh=mesh,
            in_specs=placed,
            out_specs=(P("patch", ("cfg", "section")), P("cfg", "section", None, "patch", None)),
            check_vma=False,
        )(inputs, stale_kv, q_gain, k_gain, v_gain, o_gain)

    return whole
```

```python
import functools
import math

import jax
import jax.numpy as jnp
from jax import lax
from jax.experimental import pallas as pl
from jax.experimental.pallas import tpu as pltpu
from jax.sharding import PartitionSpec as P

MESH = pl.DeviceIdType.MESH
HD = 128
MB = 8
PARTS = 4
CHUNKS = 2
SHIFT = 24.0
EPS = 1e-6
guide_scale = 6.0


def dot_nt(a, b):
    return lax.dot_general(a, b, (((1,), (1,)), ((), ())), preferred_element_type=jnp.float32)


def dot_nn(a, b):
    return lax.dot_general(a, b, (((1,), (0,)), ((), ())), preferred_element_type=jnp.float32)


def tiles(start, size):
    return pl.ds(pl.multiple_of(start, size), size)


def swapped(whole, at, piece):
    parts = [whole[:, : at.start], piece, whole[:, at.stop :]]
    parts = [part for part in parts if part.shape[1]]
    return jnp.concatenate(parts, axis=1) if len(parts) > 1 else piece


def flow(
    dims, x_ref, kv_ref, qg, kg, vg, og, fs_ref, fin_ref,
    kvb, xin, xmid, xout, gb, mask,
    kv_send, x_send, g_send, nxt_send, ret_send, fin_send,
    kv_sem, xin_sem, g_sem, fs_sem, fin_sem, rel_send, rel_sem, ret_ok, nxt_ok,
):
    heads, n_sec, n_patch, tok, width, nd, slots = dims
    quarter = n_patch // PARTS
    rows = xin.shape[1]
    per_chunk = rows // tok
    wide_keys = min(256, n_patch * tok // PARTS)
    copies = wide_keys // rows
    blocks = n_patch * tok // wide_keys
    last = n_sec // 2 - 1
    out_w = width // (2 * n_sec)
    ny = 8 if n_patch == 32 else 2
    nx = n_patch // ny
    hy = ny // 2
    c, s, p = lax.axis_index("cfg"), lax.axis_index("section"), lax.axis_index("patch")
    zh = s // 2
    core = lax.rem(s, 2)
    s0 = zh * 2
    as_int = lambda flag: flag.astype(jnp.int32)

    def patch_at(pos):
        at = lax.rem(pos, 2 * quarter)
        return (at // hy) * ny + (pos // (2 * quarter)) * hy + lax.rem(at, hy)

    def owner(h, side, branch):
        at = lax.rem(h, hy)
        return lax.rem(at + branch + 1 + h // hy, nx) * ny + side * hy + at

    x, y = p // ny, lax.rem(p, ny)
    side, at_y = y // hy, lax.rem(y, hy)
    place = x * hy + at_y
    on_core = place // quarter
    place = lax.rem(place, quarter)
    nth = lax.rem(x - at_y - c - 1 + 2 * nx + hy * nx, nx)
    is_unit = nth < heads // hy
    head = lax.rem(nth * hy + at_y, heads)
    block_at = side * 2 + core
    col = c * n_sec + s
    h_first = (out_w * col) // HD
    h_last = (out_w * col + out_w - 1) // HD
    is_final = is_unit & (zh == last)
    gains = (qg, kg, vg, og)

    bar = pltpu.get_barrier_semaphore()
    other = s0 + 1 - core

    def hello(dev):
        pl.semaphore_signal(bar, inc=1, device_id=dev, device_id_type=MESH)

    def loop(n, body, first=0):
        def step(i, _):
            body(i)
            return 0

        lax.fori_loop(first, n, step, 0)

    @pl.when(is_unit)
    def _():
        def greet_other(i):
            q = patch_at(block_at * quarter + i)

            @pl.when(q != p)
            def _():
                hello((c, other, q))

        loop(n_patch, lambda i: hello((c, s, lax.rem(p + i, n_patch))), 1)
        loop(quarter, greet_other)
        hello((c, other, p))

        @pl.when(zh < last)
        def _():
            hello((c, s + 2, p))

        for i, g in enumerate(gains):
            pltpu.make_async_copy(g.at[:, tiles(head * HD, HD)], gb.at[core, i], g_sem.at[0]).start()

    for branch in range(2):
        for n in range(slots):
            h = (h_first, h_last)[n]
            wanted = jnp.logical_not(is_final & (on_core == core) & (c == branch) & (head == h))
            if n == 1:
                wanted = wanted & (h_last > h_first)

            @pl.when(wanted)
            def _():
                hello((branch, n_sec - 2 + on_core, owner(h, side, branch)))

    unit = as_int(is_unit)
    mine_too = is_final & (on_core == core) & (head >= h_first) & (head <= h_last)
    greeted = 2 * heads + as_int(on_core != core) * (heads - unit) + as_int(is_unit & (zh > 0))
    pl.semaphore_wait(bar, greeted + as_int(is_final) * (quarter * nd) - as_int(mine_too))

    def g_copy(i):
        return pltpu.make_async_remote_copy(
            src_ref=gains[i].at[:, tiles(head * HD, HD)],
            dst_ref=gb.at[core, i],
            send_sem=g_send.at[i],
            recv_sem=g_sem.at[1],
            device_id=(c, other, p),
            device_id_type=MESH,
        )

    def x_copy(i):
        h = lax.rem(p + i, heads)
        to = owner(h, side, c)
        src = x_ref.at[:, tiles(h * HD, HD)]
        dst = xin.at[place // per_chunk, tiles(lax.rem(place, per_chunk) * tok, tok)]
        far = pltpu.make_async_remote_copy(
            src_ref=src,
            dst_ref=dst,
            send_sem=x_send.at[i],
            recv_sem=xin_sem.at[place // per_chunk],
            device_id=(c, on_core, to),
            device_id_type=MESH,
        )
        return (to == p) & (on_core == 0), src, dst, xin_sem.at[place // per_chunk], far

    def kv_copy(i):
        k = lax.rem(p + i, 8)
        h = i // 8 * 2 + lax.rem(k, 2) + lax.rem(k // 2, 2) * (heads // 2)
        to_side = k // 4
        if heads % 6:
            h, to_side = lax.rem(i, heads), i // heads
        to = owner(h, to_side, c)
        at = (side * 2 + on_core) * quarter + place
        src = kv_ref.at[:, :, tiles(h * HD, HD)]
        dst = kvb.at[core, :, tiles(at * tok, tok)]
        sem = kv_sem.at[at * tok // wide_keys]
        far = pltpu.make_async_remote_copy(
            src_ref=src,
            dst_ref=dst,
            send_sem=kv_send.at[i],
            recv_sem=sem,
            device_id=(c, s, to),
            device_id_type=MESH,
        )
        return to == p, src, dst, sem, far

    def relay(i):
        block = kvb.at[core, :, slice(i * wide_keys, (i + 1) * wide_keys)]
        return pltpu.make_async_remote_copy(
            src_ref=block,
            dst_ref=block,
            send_sem=rel_send.at[i],
            recv_sem=rel_sem.at[i],
            device_id=(c, other, p),
            device_id_type=MESH,
        )

    def start(copy):
        mine, src, dst, sem, far = copy

        @pl.when(mine)
        def _():
            pltpu.make_async_copy(src, dst, sem).start()

        @pl.when(jnp.logical_not(mine))
        def _():
            far.start()

    def sent(copy):
        @pl.when(jnp.logical_not(copy[0]))
        def _():
            copy[4].wait_send()

    first_kv = min(8, 2 * heads)
    loop(first_kv, lambda i: start(kv_copy(i)))

    @pl.when(s == 0)
    def _():
        loop(heads, lambda i: start(x_copy(i)))

    loop(2 * heads, lambda i: start(kv_copy(i)), first_kv)

    @pl.when(is_unit)
    def _():
        for i in range(4):
            g_copy(i).start()

    def ready(h):
        to = owner(h, side, c)

        @pl.when(jnp.logical_not((to == p) & (on_core == core)))
        def _():
            pl.semaphore_signal(ret_ok, inc=1, device_id=(c, s0 + on_core, to), device_id_type=MESH)

    loop(heads, ready)

    @pl.when(is_unit & (zh > 0))
    def _():
        pl.semaphore_signal(nxt_ok, inc=1, device_id=(c, s - 2, p), device_id_type=MESH)

    def next_copy(ch):
        return pltpu.make_async_remote_copy(
            src_ref=xout.at[ch],
            dst_ref=xin.at[ch],
            send_sem=nxt_send.at[ch],
            recv_sem=xin_sem.at[ch],
            device_id=(c, s + 2, p),
            device_id_type=MESH,
        )

    def ret_copy(ch, sec, i):
        to = patch_at(block_at * quarter + ch * per_chunk + i)
        src = (xin, xmid)[sec].at[ch, tiles(i * tok, tok)]
        dst = fs_ref.at[:, tiles(head * HD, HD)]
        far = pltpu.make_async_remote_copy(
            src_ref=src,
            dst_ref=dst,
            send_sem=ret_send.at[ch, sec, i],
            recv_sem=fs_sem,
            device_id=(c, s0 + sec, to),
            device_id_type=MESH,
        )
        return (to == p) & (core == sec), src, dst, fs_sem, far

    def fin_copy(ch, i, n):
        j = (HD * head) // out_w + n
        slot = head - (out_w * j) // HD
        to = patch_at(block_at * quarter + ch * per_chunk + i)
        src = xout.at[ch, tiles(i * tok, tok)]
        dst = fin_ref.at[slot, c]
        far = pltpu.make_async_remote_copy(
            src_ref=src,
            dst_ref=dst,
            send_sem=fin_send.at[ch, i, n],
            recv_sem=fin_sem.at[slot],
            device_id=(j // n_sec, lax.rem(j, n_sec), to),
            device_id_type=MESH,
        )
        return (to == p) & (j == col), src, dst, fin_sem.at[slot], far

    def attend(ch, sec, x):
        row = lambda i: gb[sec, i]
        wide = x.astype(jnp.float32)
        normed = wide * lax.rsqrt(jnp.mean(wide * wide, axis=1, keepdims=True) + EPS)
        query = (normed * row(0)).astype(jnp.bfloat16)
        key = (normed * row(1)).astype(jnp.bfloat16)
        value = (wide * row(2)).astype(jnp.bfloat16)
        near = mask[...] != 0.0
        fresh = dot_nt(query, key)
        own = slice(ch % copies * rows, (ch % copies + 1) * rows)
        diag = block_at * (CHUNKS // copies) + ch // copies
        expo = []
        for j in range(blocks):
            at = tiles(lax.rem(diag + j, blocks) * wide_keys, wide_keys)
            score = dot_nt(query, kvb[sec, 0, at])
            if j == 0:
                score = swapped(score, own, jnp.where(near, fresh, score[:, own]))
            expo.append(jnp.exp2(score * (HD**-0.5 * math.log2(math.e)) - SHIFT))
        inverse = 1.0 / jnp.sum(sum(expo), axis=1, keepdims=True)
        mixed = None
        for j in range(blocks):
            at = tiles(lax.rem(diag + j, blocks) * wide_keys, wide_keys)
            weight = expo[j] * inverse
            if j == 0:
                mixed = dot_nn(jnp.where(near, weight[:, own], 0.0).astype(jnp.bfloat16), value)
                weight = swapped(weight, own, jnp.where(near, 0.0, weight[:, own]))
            mixed = mixed + dot_nn(weight.astype(jnp.bfloat16), kvb[sec, 1, at])
        return (wide + row(3) * mixed).astype(jnp.bfloat16)

    @pl.when(is_unit)
    def _():
        blk = tok // MB
        r = lax.broadcasted_iota(jnp.int32, (rows, rows), 0)
        t = lax.broadcasted_iota(jnp.int32, (rows, rows), 1)
        seen = (r // tok == t // tok) & (t // blk <= r // blk)
        mask[...] = jnp.where(seen, 1.0, 0.0)

        def relayed():
            for i in range(blocks):
                relay(i).wait_recv()

        for i in range(blocks):
            block = kvb.at[core, :, slice(i * wide_keys, (i + 1) * wide_keys)]
            pltpu.make_async_copy(block, block, kv_sem.at[i]).wait()
            relay(i).start()
        pltpu.make_async_copy(gb.at[0], gb.at[0], g_sem.at[0]).wait()
        pltpu.make_async_copy(gb.at[1], gb.at[1], g_sem.at[1]).wait()

        for ch in range(CHUNKS):
            pltpu.make_async_copy(xin.at[ch], xin.at[ch], xin_sem.at[ch]).wait()
            if ch == 0:
                pl.when(core == 1)(relayed)
            xmid[ch] = attend(ch, 0, xin[ch])
            if ch == 0:
                pl.when(core == 0)(relayed)
            xout[ch] = attend(ch, 1, xmid[ch])

            @pl.when(zh < last)
            def _():
                if ch == 0:
                    pl.semaphore_wait(nxt_ok, 1)
                next_copy(ch).start()

            @pl.when(zh == last)
            def _():
                def go(i):
                    for n in range(nd):
                        start(fin_copy(ch, i, n))

                loop(per_chunk, go)

        pl.semaphore_wait(ret_ok, 2 * quarter - as_int(on_core == core))
        for ch in range(CHUNKS):

            def go(i):
                for sec in range(2):
                    start(ret_copy(ch, sec, i))

            loop(per_chunk, go)

        for ch in range(CHUNKS):

            @pl.when(zh < last)
            def _():
                next_copy(ch).wait_send()

            @pl.when(zh == last)
            def _():
                def go(i):
                    for n in range(nd):
                        sent(fin_copy(ch, i, n))

                loop(per_chunk, go)

            def go(i):
                for sec in range(2):
                    sent(ret_copy(ch, sec, i))

            loop(per_chunk, go)

    @pl.when(is_unit)
    def _():
        for i in range(4):
            g_copy(i).wait_send()
        for i in range(blocks):
            relay(i).wait_send()

    @pl.when(s == 0)
    def _():
        loop(heads, lambda i: sent(x_copy(i)))

    loop(2 * heads, lambda i: sent(kv_copy(i)))
    pltpu.make_async_copy(fs_ref, fs_ref, fs_sem).wait()
    pltpu.make_async_copy(fin_ref.at[0], fin_ref.at[0], fin_sem.at[0]).wait()
    if slots == 2:

        @pl.when(h_last > h_first)
        def _():
            pltpu.make_async_copy(fin_ref.at[1], fin_ref.at[1], fin_sem.at[1]).wait()


def finish(dims, fs_ref, fin_ref, kg, vg, guided_ref, fresh_ref):
    heads, n_sec, n_patch, tok, width, nd, slots = dims
    out_w = width // (2 * n_sec)
    for h in range(heads):
        at = slice(h * HD, (h + 1) * HD)
        wide = fs_ref[:, at].astype(jnp.float32)
        normed = wide * lax.rsqrt(jnp.mean(wide * wide, axis=1, keepdims=True) + EPS)
        fresh_ref[0, :, at] = (normed * kg[:, at]).astype(jnp.bfloat16)
        fresh_ref[1, :, at] = (wide * vg[:, at]).astype(jnp.bfloat16)
    parts = []
    for slot in range(slots):
        uncond = fin_ref[slot, 0].astype(jnp.float32)
        cond = fin_ref[slot, 1].astype(jnp.float32)
        parts.append(uncond + guide_scale * (cond - uncond))
    both = jnp.concatenate(parts, axis=1) if slots == 2 else parts[0]
    col = lax.axis_index("cfg") * n_sec + lax.axis_index("section")
    off = lax.rem(out_w * col, HD)
    for start in sorted({(out_w * j) % HD for j in range(2 * n_sec)}):

        @pl.when(off == start)
        def _():
            guided_ref[...] = both[:, start : start + out_w].astype(jnp.bfloat16)


def local(dims, inputs, stale_kv, q_gain, k_gain, v_gain, o_gain):
    heads, n_sec, n_patch, tok, width, nd, slots = dims
    rows = n_patch * tok // (PARTS * CHUNKS)
    per_chunk = rows // tok
    wide_keys = min(256, n_patch * tok // PARTS)
    dma = pltpu.SemaphoreType.DMA
    bf16 = jnp.bfloat16
    vmem = pl.BlockSpec(memory_space=pltpu.VMEM)
    far = pl.BlockSpec(memory_space=pl.ANY)
    fs, fin = pl.pallas_call(
        functools.partial(flow, dims),
        out_shape=(
            jax.ShapeDtypeStruct((tok, width), bf16),
            jax.ShapeDtypeStruct((slots, 2, tok, HD), bf16),
        ),
        in_specs=[far] * 6,
        out_specs=(far, far),
        scratch_shapes=[
            pltpu.VMEM((2, 2, n_patch * tok, HD), bf16),
            pltpu.VMEM((CHUNKS, rows, HD), bf16),
            pltpu.VMEM((CHUNKS, rows, HD), bf16),
            pltpu.VMEM((CHUNKS, rows, HD), bf16),
            pltpu.VMEM((2, 4, 1, HD), jnp.float32),
            pltpu.VMEM((rows, rows), jnp.float32),
            dma((2 * heads,)),
            dma((heads,)),
            dma((4,)),
            dma((CHUNKS,)),
            dma((CHUNKS, 2, per_chunk)),
            dma((CHUNKS, per_chunk, nd)),
            dma((n_patch * tok // wide_keys,)),
            dma((CHUNKS,)),
            dma((2,)),
            dma(()),
            dma((slots,)),
            dma((n_patch * tok // wide_keys,)),
            dma((n_patch * tok // wide_keys,)),
            pltpu.SemaphoreType.REGULAR,
            pltpu.SemaphoreType.REGULAR,
        ],
        compiler_params=pltpu.CompilerParams(collective_id=1, has_side_effects=True),
        name="flow",
    )(inputs[0], stale_kv[0, 0], q_gain, k_gain, v_gain, o_gain)
    guided, fresh = pl.pallas_call(
        functools.partial(finish, dims),
        out_shape=(
            jax.ShapeDtypeStruct((tok, width // (2 * n_sec)), bf16),
            jax.ShapeDtypeStruct((2, tok, width), bf16),
        ),
        in_specs=[vmem] * 4,
        out_specs=(vmem, vmem),
        name="finish",
    )(fs, fin, k_gain, v_gain)
    return guided, fresh[None, None]


def solution(mesh):
    n_cfg, n_sec, n_patch = mesh.shape["cfg"], mesh.shape["section"], mesh.shape["patch"]
    placed = (
        P("cfg", "patch", None),
        P("cfg", "section", None, "patch", None),
        P("section", None),
        P("section", None),
        P("section", None),
        P("section", None),
    )

    def whole(inputs, stale_kv, q_gain, k_gain, v_gain, o_gain):
        tok, width = inputs.shape[1] // n_patch, inputs.shape[2]
        heads = width // HD
        out_w = width // (n_cfg * n_sec)
        takers = {(HD * h + HD - 1) // out_w - (HD * h) // out_w + 1 for h in range(heads)}
        assert len(takers) == 1 and n_cfg == 2
        spans = [(out_w * j + out_w - 1) // HD - (out_w * j) // HD for j in range(n_cfg * n_sec)]
        dims = (heads, n_sec, n_patch, tok, width, takers.pop(), 1 + max(spans))
        return jax.shard_map(
            functools.partial(local, dims),
            mesh=mesh,
            in_specs=placed,
            out_specs=(P("patch", ("cfg", "section")), P("cfg", "section", None, "patch", None)),
            check_vma=False,
        )(inputs, stale_kv, q_gain, k_gain, v_gain, o_gain)

    return whole
```
